32 devices in a mesh: days: 2 (over x), sta: 16 (over z, y, core).
Axes of the slice: x: 2, y: 2, z: 4, core: 2. Of those that a mesh axis runs over, the one named last changes fastest.
Arguments:
- seismo: bfloat16 [128, 3, 1173], P(('days', 'sta')), parts along dimension 0, may hold values from -6 to 6
- waves: bfloat16 [4096, 3, 150], P('sta'), may hold values from -6 to 6
- pair_station: int32 [4096, 1], P('sta'), may hold values from 0 to 63; in each aligned block of 256 rows (0 to 255, 256 to 511, ...) at most 8 rows name the same one
- pair_template: int32 [4096], P('sta'), may hold values from 0 to 23, as said below
- chan_mask: int32 [128, 3], P(('days', 'sta')), parts along dimension 0, may hold values from 0 to 1, as said below
Outputs:
- detection: float32 [768, 1024], P(('days', 'sta')), parts along dimension 0
The draws below stay inside these ranges and needn't reach their ends.
There are 2 independent parts, one for each index of `days`. The reference program is written for one: setup_inputs(seed, part) draws one part's arguments, and reference() takes and returns one part's arrays. A program takes and returns all parts, laid end to end along the dimension named above; an argument that names none is the same for every part. Nothing has to cross between parts.
Inputs may be any that keep to these rules, and one draw needn't show every extreme that they name: `pair_station`: within the rows of one device (aligned blocks of 256 rows) no station is named more than 8 times, a bound that some block reaches. `pair_template`: within the rows of one device the numbers never fall and each of the 24 numbers appears at least once. `chan_mask`: every station has at least one available component.
All inputs are finite; a program needn't handle non-finite values.
Results may differ from the reference program's by a relative error of at most 0.0029.
Values may be sent and summed in bfloat16 or wider, within the bound.
A program may use at most 128 MiB of HBM per device.

```python
import math
import jax
import jax.numpy as jnp
import numpy as np
from jax import lax

COMP = 3
L = 150
PAIR_DEV = 256
K_DEV = 24
STATIONS = 64
PAIRS = 4096
CAP = 8
SAMPLES = 1173
N_STA = 16


def draw_pair_template(key, part):
    key = jax.random.fold_in(key, 11)
    block_count = PAIRS // PAIR_DEV
    block_keys = jax.random.split(key, block_count)

    def one_block(block_key):
        shuffled = jax.random.permutation(block_key, PAIR_DEV - 1) + 1
        cut_points = jnp.sort(shuffled[:K_DEV - 1])
        position = jnp.arange(PAIR_DEV)
        return jnp.sum((cut_points[None, :] <= position[:, None]).astype(jnp.int32), axis=1)
    return jax.vmap(one_block)(block_keys).reshape(PAIRS).astype(jnp.int32)


def draw_chan_mask(key, part):
    key = jax.random.fold_in(key, 23)
    first_key, second_key = jax.random.split(key)
    rolled = jax.random.randint(first_key, (STATIONS, COMP), 0, 5)
    forced = jax.random.randint(second_key, (STATIONS,), 0, COMP)
    chosen = jnp.arange(COMP)[None, :] == forced[:, None]
    return jnp.maximum((rolled > 0).astype(jnp.int32), chosen.astype(jnp.int32)).astype(jnp.int32)


def block_scale(key, dims, cuts, least, high):
    def one(dim, blocks):
        draws = jax.random.uniform(jax.random.fold_in(jax.random.fold_in(key, 6), dim), (blocks,), jnp.float32, least / len(cuts), high / len(cuts))
        return jnp.repeat(jnp.exp(draws), dims[dim] // blocks).reshape((-1,) + (1,) * (len(dims) - dim - 1))

    factor_of = one(*cuts[0])
    for cut in cuts[1:]:
        factor_of = factor_of * one(*cut)
    return factor_of


def deal_out(rng, own, number, rows, count, top, most, skew):
    sequence = jax.random.permutation(rng, count)
    crowded, ordinary = portions_of(count, rows * top, most, skew, True), portions_of(count, rows * top, most, skew, False)
    places = jnp.arange(count)

    def named(tallies, rotation):
        used = int((tallies > 0).sum())
        fixed = max(1, used // 4)
        moved = fixed + (places - fixed + rotation * (used - fixed)) % max(1, count - fixed)
        return jnp.zeros((count,), jnp.int32).at[sequence[jnp.where(places < fixed, places, moved)]].set(jnp.asarray(tallies, jnp.int32))

    tallies = jnp.where(number % 4 == 0, named(crowded, number // 4), named(ordinary, number - number // 4 - 1))
    mixed = jax.random.permutation(jax.random.fold_in(own, 3), count)
    source_of, sink = mixed[0:count // 2 * 2:2], mixed[1:count // 2 * 2:2]
    room = jnp.minimum(tallies[source_of] - 1, most - tallies[sink]) // 2
    room = jnp.where((source_of == sequence[0]) | (sink == sequence[0]) | (tallies[sink] == 0), 0, jnp.maximum(room, 0))
    moved = jax.random.randint(jax.random.fold_in(own, 4), (count // 2,), 0, 1 << 20) % (room + 1)
    tallies = tallies.at[source_of].add(-moved).at[sink].add(moved)
    members = jnp.searchsorted(jnp.cumsum(tallies), jnp.arange(rows * top), side="right").astype(jnp.int32)
    table = members.reshape(top, rows).T
    table = table[jax.random.permutation(jax.random.fold_in(own, 1), rows)]
    rotation = jax.random.randint(jax.random.fold_in(own, 2), (rows, 1), 0, top)
    return jnp.take_along_axis(table, (jnp.arange(top)[None, :] + rotation) % top, axis=1)


def portions_of(amount, total, reach, slope, full):
    weights = [(1 << 20) // math.isqrt(rank ** slope) + 1 for rank in range(1, amount + 1)]
    largest = reach if full else min(reach, max(-(-total // amount), total * weights[0] // sum(weights)))
    least = 1 if total - largest >= amount - 1 else 0
    holding, spare = [largest] + [least] * (amount - 1), total - largest - least * (amount - 1)
    while spare > 0:
        free = [i for i in range(1, amount) if holding[i] < largest] or [i for i in range(1, amount) if holding[i] < reach]
        whole, remaining = sum([weights[i] for i in free]), spare
        for i in free:
            addition = min(reach - holding[i], max(1, remaining * weights[i] // whole), spare)
            holding[i] = holding[i] + addition
            spare = spare - addition
    return np.array(holding)


def normal_values(key, shape, spread, reach, cuts=(), held_as=jnp.bfloat16):
    loudness = block_scale(key, shape, cuts, -0.22, 0.18) if cuts else 1.0
    result = jax.random.normal(key, shape, jnp.float32) * spread * loudness
    return jnp.minimum(jnp.maximum(result, -reach), reach).astype(held_as)


def setup_inputs(seed: int = 0, part: int = 0) -> dict:
    keys = jax.random.split(jax.random.key(seed), 6)
    part_keys = jax.random.split(jax.random.fold_in(keys[5], part), 6)
    seismo = normal_values(part_keys[0], (STATIONS, COMP, SAMPLES), 1.0, 6.0, ((0, 16),))
    waves = normal_values(keys[1], (PAIRS, COMP, L), 1.0, 6.0, ((0, 16),))
    pair_station_keys = jax.random.split(jax.random.fold_in(keys[2], 1), PAIRS // PAIR_DEV)
    pair_station_turns = jax.random.permutation(jax.random.fold_in(keys[2], 3), PAIRS // PAIR_DEV)
    pair_station = jax.vmap(lambda own, number: deal_out(jax.random.fold_in(keys[2], 2), own, number, PAIR_DEV, STATIONS, 1, CAP, 2))(pair_station_keys, pair_station_turns).reshape((PAIRS, 1))
    pair_template = draw_pair_template(jax.random.fold_in(keys[5], 71), part)
    chan_mask = draw_chan_mask(jax.random.fold_in(jax.random.fold_in(keys[5], part), 71), part)
    return {"seismo": seismo, "waves": waves, "pair_station": pair_station, "pair_template": pair_template, "chan_mask": chan_mask}


epsilon = 1e-06

def reference(seismo, waves, pair_station, pair_template, chan_mask):
    pair_total, comp_count, length = waves.shape
    samples = seismo.shape[2]
    lag_count = samples - length + 1
    station = pair_station[:, 0].astype(jnp.int32)
    template_id = (jnp.arange(pair_total) // PAIR_DEV * K_DEV + pair_template).astype(jnp.int32)
    by_station = jnp.argsort(station, stable=True).astype(jnp.int32)
    sorted_station = station[by_station]
    first_row = jnp.searchsorted(sorted_station, jnp.arange(STATIONS)).astype(jnp.int32)
    slot_rank = (jnp.arange(pair_total) - first_row[sorted_station]).astype(jnp.int32)
    table = jnp.full((STATIONS, N_STA * CAP), -1, jnp.int32).at[sorted_station, slot_rank].set(by_station)

    def step(summed, scan_entry):
        station_index, slot_rows = scan_entry
        is_live = slot_rows >= 0
        safe_rows = jnp.maximum(slot_rows, 0)
        wave_float = jnp.take(waves, safe_rows, axis=0).astype(jnp.float32)
        station_trace = lax.dynamic_index_in_dim(seismo, station_index, 0, keepdims=False).astype(jnp.float32)
        windows = jnp.stack([station_trace[:, offset:offset + lag_count] for offset in range(length)], axis=1)
        energy = lax.optimization_barrier(jnp.sum(jnp.square(windows), axis=1))
        product = jnp.einsum('mcl,cln->mcn', wave_float, windows, precision=lax.Precision.HIGHEST)
        live_mask = lax.dynamic_index_in_dim(chan_mask, station_index, 0, keepdims=False).astype(jnp.float32)
        wave_scale = lax.rsqrt(lax.optimization_barrier(jnp.sum(jnp.square(wave_float), axis=2)) + epsilon)
        data_scale = live_mask[:, None] * lax.rsqrt(energy + epsilon)
        scores = lax.optimization_barrier(jnp.sum(product * wave_scale[:, :, None] * data_scale[None, :, :], axis=1)).astype(jnp.bfloat16)
        template_rows = jnp.take(template_id, safe_rows)
        added = jnp.where(is_live[:, None], scores.astype(jnp.float32), jnp.zeros((), jnp.float32))
        summed = summed.at[template_rows].add(added)
        return (summed, None)
    start = jnp.zeros((N_STA * K_DEV, lag_count), jnp.float32)
    detection, unused = lax.scan(step, start, (jnp.arange(STATIONS, dtype=jnp.int32), table))
    return detection
```

```python
import functools

import jax
import jax.numpy as jnp
from jax import lax
from jax.experimental import pallas as pl
from jax.experimental.pallas import tpu as pltpu
from jax.sharding import PartitionSpec as P

K_DEV = 24
SLOTS = 8
PHASES = 8
LANES = 128
WIDE = 256
MESH = pl.DeviceIdType.MESH

epsilon = 1e-06


def dot(a, b):
    return jnp.dot(a, b, preferred_element_type=jnp.float32)


def iota(shape, dim):
    return lax.broadcasted_iota(jnp.int32, shape, dim)


def kernel(
    peers, stations, comps, length,
    seismo_ref, waves_ref, station_ref, template_ref, mask_ref, out_ref,
    got, shifted, chooser, filt, wave_scale, scores, order, send_sem, recv_sem,
):
    f32, bf16 = jnp.float32, jnp.bfloat16
    me = lax.axis_index("sta")
    traces = stations * comps
    samples = seismo_ref.shape[1]
    pairs = waves_ref.shape[0]
    slot_total = peers * stations * SLOTS
    taps = -(-(length + PHASES - 1) // 16) * 16
    steps = taps // PHASES
    per_tail = LANES // steps
    tail_groups = -(-traces // per_tail)
    head_rows = traces * PHASES

    barrier = pltpu.get_barrier_semaphore()

    def greet(i, carry):
        pl.semaphore_signal(
            barrier, inc=1, device_id={"sta": lax.rem(me + i, peers)}, device_id_type=MESH
        )
        return carry

    lax.fori_loop(1, peers, greet, 0)

    pick = (iota((head_rows, traces), 0) // PHASES == iota((head_rows, traces), 1)).astype(f32)
    pick = (pick * mask_ref[...].astype(f32)).astype(bf16)
    spread = dot(pick, seismo_ref[...])
    same_phase = iota((head_rows, samples), 1) % PHASES == iota((head_rows, samples), 0) % PHASES
    spread = jnp.where(same_phase, spread, 0.0).astype(bf16)
    head_pick = (iota((samples, LANES), 0) // PHASES == iota((samples, LANES), 1)).astype(bf16)
    head = dot(spread, head_pick)
    first = PHASES * LANES
    left = samples - first
    tail_pick = (
        iota((left, LANES), 0) // PHASES == iota((left, LANES), 1) % steps
    ).astype(bf16)
    tails = dot(spread[:, first:], tail_pick)
    place = iota((head_rows, LANES), 0) // PHASES % per_tail == iota((head_rows, LANES), 1) // steps
    tails = jnp.where(place, tails, 0.0)
    parts = [head]
    for g in range(tail_groups):
        part = None
        for j in range(g * per_tail, min(traces, (g + 1) * per_tail)):
            one = tails[j * PHASES:(j + 1) * PHASES]
            part = one if part is None else part + one
        parts.append(part)
    if tail_groups % 2:
        parts.append(jnp.zeros((PHASES, LANES), f32))
    got[me] = jnp.concatenate(parts, axis=0).astype(bf16)

    pl.semaphore_wait(barrier, peers - 1)

    def offset(k):
        odd = k % 2
        return odd * ((k + 1) // 2) + (1 - odd) * (peers - k // 2)

    def transfer(k, source):
        return pltpu.make_async_remote_copy(
            src_ref=got.at[source],
            dst_ref=got.at[source],
            send_sem=send_sem.at[k],
            recv_sem=recv_sem.at[source],
            device_id={"sta": lax.rem(me + offset(k), peers)},
            device_id_type=MESH,
        )

    def push(k, carry):
        transfer(k, me).start()
        return carry

    lax.fori_loop(1, peers, push, 0)

    diagonal = iota((pairs, pairs), 0) == iota((pairs, pairs), 1)
    station_column = station_ref[...]
    station_row = jnp.sum(jnp.where(diagonal, station_column, 0), axis=0, keepdims=True)
    earlier = iota((pairs, pairs), 0) < iota((pairs, pairs), 1)
    matched = (station_column == station_row) & earlier
    rank = jnp.sum(matched.astype(jnp.int32), axis=0, keepdims=True)
    slot = station_row * SLOTS + rank
    chooser[...] = (iota((slot_total, pairs), 0) == slot).astype(bf16)

    for c in range(comps):
        lanes = slice(c * WIDE, (c + 1) * WIDE)
        wave = waves_ref[:, lanes].astype(f32)
        for d in range(PHASES):
            moved = wave if d == 0 else pltpu.roll(wave, d, 1)
            shifted[d, :, lanes] = moved.astype(bf16)

    chunk = 128
    blocks = chunk // SLOTS

    def gather(i, carry):
        rows = chooser[pl.ds(pl.multiple_of(i * chunk, chunk), chunk), :]
        for d in range(0, PHASES, 2):
            low = dot(rows, shifted[d])
            high = dot(rows, shifted[d + 1])
            if d == 0:
                for c in range(comps):
                    energy = jnp.sum(
                        jnp.square(low[:, c * WIDE:(c + 1) * WIDE]), axis=1, keepdims=True
                    )
                    wave_scale[
                        pl.ds(pl.multiple_of(i * chunk, chunk), chunk),
                        c * LANES:(c + 1) * LANES,
                    ] = jnp.broadcast_to(lax.rsqrt(energy + epsilon), (chunk, LANES))
            both = jnp.concatenate(
                [low.reshape(blocks, SLOTS, -1), high.reshape(blocks, SLOTS, -1)], axis=1
            )
            filt[pl.ds(i * blocks, blocks), d * SLOTS:(d + 2) * SLOTS, :] = both.astype(bf16)
        return carry

    lax.fori_loop(0, slot_total // chunk, gather, 0)

    tap, phase = iota((16, taps), 1), iota((16, taps), 0)
    band = ((tap >= phase) & (tap < phase + length)).astype(bf16)
    lane = iota((PHASES, LANES), 1)

    def correlate(k, carry):
        peer = lax.rem(me + 2 * peers - offset(k), peers)

        @pl.when(k > 0)
        def _():
            transfer(k, peer).wait_recv()

        block = got[peer].astype(f32)

        def one_station(s):
            total = None
            for c in range(comps):
                j = s * comps + c
                head = block[j * PHASES:(j + 1) * PHASES]
                group = head_rows + j // per_tail * PHASES
                tail = block[group:group + PHASES]
                rows = [head]
                for q in range(1, steps):
                    begin = pltpu.roll(head, LANES - q, 1)
                    end = pltpu.roll(tail, (LANES - q - steps * (j % per_tail)) % LANES, 1)
                    rows.append(jnp.where(lane < LANES - q, begin, end))
                data = jnp.concatenate(rows, axis=0).astype(bf16)
                product = dot(filt[peer * stations + s, :, c * WIDE:c * WIDE + taps], data)
                energy = dot(band, data * data)[:PHASES]
                data_scale = lax.rsqrt(energy + epsilon)
                start = pl.multiple_of((peer * stations + s) * SLOTS, SLOTS)
                scale = wave_scale[pl.ds(start, SLOTS), c * LANES:(c + 1) * LANES]
                factor = data_scale[:, None, :] * scale[None, :, :]
                term = product.reshape(PHASES, SLOTS, LANES) * factor
                total = term if total is None else total + term
            return total

        for s in range(0, stations, 2):
            low, high = one_station(s), one_station(s + 1)
            start = pl.multiple_of((peer * stations + s) * SLOTS, 2 * SLOTS)
            for d in range(PHASES):
                scores[pl.ds(start, 2 * SLOTS), d * LANES:(d + 1) * LANES] = jnp.concatenate(
                    [low[d], high[d]], axis=0
                ).astype(bf16)
        return carry

    lax.fori_loop(0, peers, correlate, 0)

    lags = PHASES * LANES
    for d in range(PHASES):
        order[d * LANES:(d + 1) * LANES, :] = (
            iota((LANES, lags), 1) == PHASES * iota((LANES, lags), 0) + d
        ).astype(bf16)
    member = (iota((32, pairs), 0) == template_ref[...]).astype(bf16)
    combine = lax.dot_general(
        member, chooser[...], (((1,), (1,)), ((), ())), preferred_element_type=f32
    ).astype(bf16)
    found = dot(combine, scores[...])
    coarse = found.astype(bf16)
    fine = (found - coarse.astype(f32)).astype(bf16)
    out = dot(coarse, order[...]) + dot(fine, order[...])
    out_ref[...] = out[:K_DEV]

    def drain(k, carry):
        transfer(k, me).wait_send()
        return carry

    lax.fori_loop(1, peers, drain, 0)


def per_device(peers, seismo, waves, pair_station, pair_template, chan_mask):
    stations, comps, samples = seismo.shape
    pairs, _, length = waves.shape
    lags = samples - length + 1
    assert lags == PHASES * LANES
    assert 2 * pairs // (stations * peers) <= SLOTS
    slot_total = peers * stations * SLOTS
    steps = -(-(length + PHASES - 1) // 16) * 16 // PHASES
    tail_groups = -(-stations * comps // (LANES // steps))
    rows = -(-(stations * comps + tail_groups) // 2) * 2 * PHASES
    wide = jnp.pad(waves, ((0, 0), (0, 0), (0, WIDE - length))).reshape(pairs, comps * WIDE)
    vmem = pl.BlockSpec(memory_space=pltpu.VMEM)
    bf16 = jnp.bfloat16
    return pl.pallas_call(
        functools.partial(kernel, peers, stations, comps, length),
        out_shape=jax.ShapeDtypeStruct((K_DEV, lags), jnp.float32),
        in_specs=[vmem] * 5,
        out_specs=vmem,
        scratch_shapes=[
            pltpu.VMEM((peers, rows, LANES), bf16),
            pltpu.VMEM((PHASES, pairs, comps * WIDE), bf16),
            pltpu.VMEM((slot_total, pairs), bf16),
            pltpu.VMEM((peers * stations, PHASES * SLOTS, comps * WIDE), bf16),
            pltpu.VMEM((slot_total, comps * LANES), jnp.float32),
            pltpu.VMEM((slot_total, lags), bf16),
            pltpu.VMEM((lags, lags), bf16),
            pltpu.SemaphoreType.DMA((peers,)),
            pltpu.SemaphoreType.DMA((peers,)),
        ],
        compiler_params=pltpu.CompilerParams(
            collective_id=0, has_side_effects=True, vmem_limit_bytes=56 * 1024 * 1024
        ),
    )(
        seismo.reshape(stations * comps, samples),
        wide,
        pair_station,
        pair_template.reshape(1, pairs),
        chan_mask.reshape(1, stations * comps),
    )


def solution(mesh):
    return jax.shard_map(
        functools.partial(per_device, mesh.shape["sta"]),
        mesh=mesh,
        in_specs=(
            P(("days", "sta"), None, None),
            P("sta", None, None),
            P("sta", None),
            P("sta"),
            P(("days", "sta"), None),
        ),
        out_specs=P(("days", "sta"), None),
        check_vma=False,
    )
```

```python
import functools

import jax
import jax.numpy as jnp
from jax import lax
from jax.experimental import pallas as pl
from jax.experimental.pallas import tpu as pltpu
from jax.sharding import PartitionSpec as P

K_DEV = 24
SLOTS = 8
PHASES = 8
LANES = 128
WIDE = 256
MESH = pl.DeviceIdType.MESH

epsilon = 1e-06


def dot(a, b):
    return jnp.dot(a, b, preferred_element_type=jnp.float32)


def iota(shape, dim):
    return lax.broadcasted_iota(jnp.int32, shape, dim)


def kernel(
    peers, stations, comps, length,
    seismo_ref, waves_ref, station_ref, template_ref, mask_ref, out_ref,
    got, shifted, chooser, filt, wave_scale, scores, order, send_sem, recv_sem,
):
    f32, bf16 = jnp.float32, jnp.bfloat16
    me = lax.axis_index("sta")
    traces = stations * comps
    samples = seismo_ref.shape[2]
    pairs = waves_ref.shape[2]
    slot_total = peers * stations * SLOTS
    taps = -(-(length + PHASES - 1) // 16) * 16
    steps = taps // PHASES
    per_tail = LANES // steps
    tail_groups = -(-traces // per_tail)
    head_rows = traces * PHASES

    barrier = pltpu.get_barrier_semaphore()

    def greet(i, carry):
        pl.semaphore_signal(
            barrier, inc=1, device_id={"sta": lax.rem(me + i, peers)}, device_id_type=MESH
        )
        return carry

    lax.fori_loop(1, peers, greet, 0)

    spread = None
    for c in range(comps):
        source = iota((head_rows, stations), 0) // PHASES
        pick = (source == iota((head_rows, stations), 1) * comps + c).astype(bf16)
        record = seismo_ref[c].astype(f32) * mask_ref[:, c:c + 1].astype(f32)
        one = dot(pick, record.astype(bf16))
        spread = one if spread is None else spread + one
    same_phase = iota((head_rows, samples), 1) % PHASES == iota((head_rows, samples), 0) % PHASES
    spread = jnp.where(same_phase, spread, 0.0).astype(bf16)
    head_pick = (iota((samples, LANES), 0) // PHASES == iota((samples, LANES), 1)).astype(bf16)
    head = dot(spread, head_pick)
    first = PHASES * LANES
    left = samples - first
    tail_pick = (
        iota((left, LANES), 0) // PHASES == iota((left, LANES), 1) % steps
    ).astype(bf16)
    tails = dot(spread[:, first:], tail_pick)
    place = iota((head_rows, LANES), 0) // PHASES % per_tail == iota((head_rows, LANES), 1) // steps
    tails = jnp.where(place, tails, 0.0)
    parts = [head]
    for g in range(tail_groups):
        part = None
        for j in range(g * per_tail, min(traces, (g + 1) * per_tail)):
            one = tails[j * PHASES:(j + 1) * PHASES]
            part = one if part is None else part + one
        parts.append(part)
    if tail_groups % 2:
        parts.append(jnp.zeros((PHASES, LANES), f32))
    got[me] = jnp.concatenate(parts, axis=0).astype(bf16)

    pl.semaphore_wait(barrier, peers - 1)

    def offset(k):
        odd = k % 2
        return odd * ((k + 1) // 2) + (1 - odd) * (peers - k // 2)

    def transfer(k, source):
        return pltpu.make_async_remote_copy(
            src_ref=got.at[source],
            dst_ref=got.at[source],
            send_sem=send_sem.at[k],
            recv_sem=recv_sem.at[source],
            device_id={"sta": lax.rem(me + offset(k), peers)},
            device_id_type=MESH,
        )

    def push(k, carry):
        transfer(k, me).start()
        return carry

    lax.fori_loop(1, peers, push, 0)

    diagonal = iota((pairs, pairs), 0) == iota((pairs, pairs), 1)
    station_row = station_ref[...]
    station_column = jnp.sum(jnp.where(diagonal, station_row, 0), axis=1, keepdims=True)
    earlier = iota((pairs, pairs), 0) < iota((pairs, pairs), 1)
    matched = (station_column == station_row) & earlier
    rank = jnp.sum(matched.astype(jnp.int32), axis=0, keepdims=True)
    slot = station_row * SLOTS + rank
    chooser[...] = (iota((slot_total, pairs), 0) == slot).astype(bf16)

    for c in range(comps):
        wave = jnp.concatenate(
            [waves_ref[c].astype(f32), jnp.zeros((taps - length, pairs), f32)], axis=0
        )
        for d in range(PHASES):
            moved = wave if d == 0 else pltpu.roll(wave, d, 0)
            shifted[d, c] = moved.astype(bf16)

    chunk = 128
    blocks = chunk // SLOTS

    def gather(i, carry):
        span = pl.ds(pl.multiple_of(i * chunk, chunk), chunk)
        rows = chooser[span, :]
        for c in range(comps):
            for d in range(0, PHASES, 2):
                low, high = [
                    lax.dot_general(
                        rows, shifted[d + e, c], (((1,), (1,)), ((), ())),
                        preferred_element_type=f32,
                    )
                    for e in range(2)
                ]
                if d == 0:
                    energy = jnp.sum(jnp.square(low), axis=1, keepdims=True)
                    wave_scale[span, c * LANES:(c + 1) * LANES] = jnp.broadcast_to(
                        lax.rsqrt(energy + epsilon), (chunk, LANES)
                    )
                both = jnp.concatenate(
                    [low.reshape(blocks, SLOTS, taps), high.reshape(blocks, SLOTS, taps)], axis=1
                )
                filt[
                    pl.ds(i * blocks, blocks), d * SLOTS:(d + 2) * SLOTS,
                    c * WIDE:c * WIDE + taps,
                ] = both.astype(bf16)
        return carry

    lax.fori_loop(0, slot_total // chunk, gather, 0)

    tap, phase = iota((16, taps), 1), iota((16, taps), 0)
    band = ((tap >= phase) & (tap < phase + length)).astype(bf16)
    lane = iota((PHASES, LANES), 1)

    def correlate(k, carry):
        peer = lax.rem(me + 2 * peers - offset(k), peers)

        @pl.when(k > 0)
        def _():
            transfer(k, peer).wait_recv()

        block = got[peer].astype(f32)

        def one_station(s):
            total = None
            for c in range(comps):
                j = s * comps + c
                head = block[j * PHASES:(j + 1) * PHASES]
                group = head_rows + j // per_tail * PHASES
                tail = block[group:group + PHASES]
                rows = [head]
                for q in range(1, steps):
                    begin = pltpu.roll(head, LANES - q, 1)
                    end = pltpu.roll(tail, (LANES - q - steps * (j % per_tail)) % LANES, 1)
                    rows.append(jnp.where(lane < LANES - q, begin, end))
                data = jnp.concatenate(rows, axis=0).astype(bf16)
                product = dot(filt[peer * stations + s, :, c * WIDE:c * WIDE + taps], data)
                energy = dot(band, data * data)[:PHASES]
                data_scale = lax.rsqrt(energy + epsilon)
                start = pl.multiple_of((peer * stations + s) * SLOTS, SLOTS)
                scale = wave_scale[pl.ds(start, SLOTS), c * LANES:(c + 1) * LANES]
                factor = data_scale[:, None, :] * scale[None, :, :]
                term = product.reshape(PHASES, SLOTS, LANES) * factor
                total = term if total is None else total + term
            return total

        for s in range(0, stations, 2):
            low, high = one_station(s), one_station(s + 1)
            start = pl.multiple_of((peer * stations + s) * SLOTS, 2 * SLOTS)
            for d in range(PHASES):
                scores[pl.ds(start, 2 * SLOTS), d * LANES:(d + 1) * LANES] = jnp.concatenate(
                    [low[d], high[d]], axis=0
                ).astype(bf16)
        return carry

    lax.fori_loop(0, peers, correlate, 0)

    lags = PHASES * LANES
    for d in range(PHASES):
        order[d * LANES:(d + 1) * LANES, :] = (
            iota((LANES, lags), 1) == PHASES * iota((LANES, lags), 0) + d
        ).astype(bf16)
    member = (iota((32, pairs), 0) == template_ref[...]).astype(bf16)
    combine = lax.dot_general(
        member, chooser[...], (((1,), (1,)), ((), ())), preferred_element_type=f32
    ).astype(bf16)
    found = dot(combine, scores[...])
    coarse = found.astype(bf16)
    fine = (found - coarse.astype(f32)).astype(bf16)
    out = dot(coarse, order[...]) + dot(fine, order[...])
    out_ref[...] = out[:K_DEV]

    def drain(k, carry):
        transfer(k, me).wait_send()
        return carry

    lax.fori_loop(1, peers, drain, 0)


def per_device(peers, seismo, waves, pair_station, pair_template, chan_mask):
    stations, comps, samples = seismo.shape
    pairs, _, length = waves.shape
    lags = samples - length + 1
    assert lags == PHASES * LANES
    assert 2 * pairs // (stations * peers) <= SLOTS
    slot_total = peers * stations * SLOTS
    steps = -(-(length + PHASES - 1) // 16) * 16 // PHASES
    tail_groups = -(-stations * comps // (LANES // steps))
    rows = -(-(stations * comps + tail_groups) // 2) * 2 * PHASES
    vmem = pl.BlockSpec(memory_space=pltpu.VMEM)
    bf16 = jnp.bfloat16
    return pl.pallas_call(
        functools.partial(kernel, peers, stations, comps, length),
        out_shape=jax.ShapeDtypeStruct((K_DEV, lags), jnp.float32),
        in_specs=[vmem] * 5,
        out_specs=vmem,
        scratch_shapes=[
            pltpu.VMEM((peers, rows, LANES), bf16),
            pltpu.VMEM((PHASES, comps, steps * PHASES, pairs), bf16),
            pltpu.VMEM((slot_total, pairs), bf16),
            pltpu.VMEM((peers * stations, PHASES * SLOTS, comps * WIDE), bf16),
            pltpu.VMEM((slot_total, comps * LANES), jnp.float32),
            pltpu.VMEM((slot_total, lags), bf16),
            pltpu.VMEM((lags, lags), bf16),
            pltpu.SemaphoreType.DMA((peers,)),
            pltpu.SemaphoreType.DMA((peers,)),
        ],
        compiler_params=pltpu.CompilerParams(
            collective_id=0, has_side_effects=True, vmem_limit_bytes=56 * 1024 * 1024
        ),
    )(
        jnp.transpose(seismo, (1, 0, 2)),
        jnp.transpose(waves, (1, 2, 0)),
        pair_station.reshape(1, pairs),
        pair_template.reshape(1, pairs),
        chan_mask,
    )


def solution(mesh):
    return jax.shard_map(
        functools.partial(per_device, mesh.shape["sta"]),
        mesh=mesh,
        in_specs=(
            P(("days", "sta"), None, None),
            P("sta", None, None),
            P("sta", None),
            P("sta"),
            P(("days", "sta"), None),
        ),
        out_specs=P(("days", "sta"), None),
        check_vma=False,
    )
```

```python
import functools

import jax
import jax.numpy as jnp
from jax import lax
from jax.experimental import pallas as pl
from jax.experimental.pallas import tpu as pltpu
from jax.sharding import PartitionSpec as P

K_DEV = 24
SLOTS = 8
PHASES = 8
LANES = 128
WIDE = 256
MESH = pl.DeviceIdType.MESH

epsilon = 1e-06


def dot(a, b):
    return jnp.dot(a, b, preferred_element_type=jnp.float32)


def iota(shape, dim):
    return lax.broadcasted_iota(jnp.int32, shape, dim)


def kernel(
    peers, stations, comps, length,
    seismo_ref, waves_ref, station_ref, template_ref, mask_ref, out_ref,
    got, shifted, chooser, filt, wave_scale, scores, order, send_sem, recv_sem,
):
    f32, bf16 = jnp.float32, jnp.bfloat16
    me = lax.axis_index("sta")
    traces = stations * comps
    samples = seismo_ref.shape[2]
    pairs = waves_ref.shape[2]
    slot_total = peers * stations * SLOTS
    taps = -(-(length + PHASES - 1) // 16) * 16
    steps = taps // PHASES
    per_tail = LANES // steps
    tail_groups = -(-traces // per_tail)
    head_rows = traces * PHASES

    barrier = pltpu.get_barrier_semaphore()

    def greet(i, carry):
        pl.semaphore_signal(
            barrier, inc=1, device_id={"sta": lax.rem(me + i, peers)}, device_id_type=MESH
        )
        return carry

    lax.fori_loop(1, peers, greet, 0)

    spread = None
    for c in range(comps):
        source = iota((head_rows, stations), 0) // PHASES
        pick = (source == iota((head_rows, stations), 1) * comps + c).astype(bf16)
        record = seismo_ref[c].astype(f32) * mask_ref[:, c:c + 1].astype(f32)
        one = dot(pick, record.astype(bf16))
        spread = one if spread is None else spread + one
    same_phase = iota((head_rows, samples), 1) % PHASES == iota((head_rows, samples), 0) % PHASES
    spread = jnp.where(same_phase, spread, 0.0).astype(bf16)
    head_pick = (iota((samples, LANES), 0) // PHASES == iota((samples, LANES), 1)).astype(bf16)
    head = dot(spread, head_pick)
    first = PHASES * LANES
    left = samples - first
    tail_pick = (
        iota((left, LANES), 0) // PHASES == iota((left, LANES), 1) % steps
    ).astype(bf16)
    tails = dot(spread[:, first:], tail_pick)
    place = iota((head_rows, LANES), 0) // PHASES % per_tail == iota((head_rows, LANES), 1) // steps
    tails = jnp.where(place, tails, 0.0)
    parts = [head]
    for g in range(tail_groups):
        part = None
        for j in range(g * per_tail, min(traces, (g + 1) * per_tail)):
            one = tails[j * PHASES:(j + 1) * PHASES]
            part = one if part is None else part + one
        parts.append(part)
    if tail_groups % 2:
        parts.append(jnp.zeros((PHASES, LANES), f32))
    got[me] = jnp.concatenate(parts, axis=0).astype(bf16)

    def offset(k):
        odd = k % 2
        return odd * ((k + 1) // 2) + (1 - odd) * (peers - k // 2)

    def transfer(k, source):
        return pltpu.make_async_remote_copy(
            src_ref=got.at[source],
            dst_ref=got.at[source],
            send_sem=send_sem.at[k],
            recv_sem=recv_sem.at[source],
            device_id={"sta": lax.rem(me + offset(k), peers)},
            device_id_type=MESH,
        )

    diagonal = iota((pairs, pairs), 0) == iota((pairs, pairs), 1)
    station_row = station_ref[...]
    station_column = jnp.sum(jnp.where(diagonal, station_row, 0), axis=1, keepdims=True)
    earlier = iota((pairs, pairs), 0) < iota((pairs, pairs), 1)
    matched = (station_column == station_row) & earlier
    rank = jnp.sum(matched.astype(jnp.int32), axis=0, keepdims=True)
    slot = station_row * SLOTS + rank
    chooser[...] = (iota((slot_total, pairs), 0) == slot).astype(bf16)

    for c in range(comps):
        wave = jnp.concatenate(
            [waves_ref[c].astype(f32), jnp.zeros((taps - length, pairs), f32)], axis=0
        )
        for d in range(PHASES):
            moved = wave if d == 0 else pltpu.roll(wave, d, 0)
            shifted[d, c] = moved.astype(bf16)

    lags = PHASES * LANES
    for d in range(PHASES):
        order[d * LANES:(d + 1) * LANES, :] = (
            iota((LANES, lags), 1) == PHASES * iota((LANES, lags), 0) + d
        ).astype(bf16)
    member = (iota((32, pairs), 0) == template_ref[...]).astype(bf16)
    combine = lax.dot_general(
        member, chooser[...], (((1,), (1,)), ((), ())), preferred_element_type=f32
    ).astype(bf16)
    pl.semaphore_wait(barrier, peers - 1)

    def push(k, carry):
        transfer(k, me).start()
        return carry

    lax.fori_loop(1, peers, push, 0)

    chunk = min(2 * pairs, slot_total)
    blocks = chunk // SLOTS

    def gather(i, carry):
        span = pl.ds(pl.multiple_of(i * chunk, chunk), chunk)
        rows = chooser[span, :]
        for c in range(comps):
            for d in range(0, PHASES, 2):
                low, high = [
                    lax.dot_general(
                        rows, shifted[d + e, c], (((1,), (1,)), ((), ())),
                        preferred_element_type=f32,
                    )
                    for e in range(2)
                ]
                if d == 0:
                    energy = jnp.sum(jnp.square(low), axis=1, keepdims=True)
                    wave_scale[span, c * LANES:(c + 1) * LANES] = jnp.broadcast_to(
                        lax.rsqrt(energy + epsilon), (chunk, LANES)
                    )
                both = jnp.concatenate(
                    [low.reshape(blocks, SLOTS, taps), high.reshape(blocks, SLOTS, taps)], axis=1
                )
                filt[
                    pl.ds(i * blocks, blocks), d * SLOTS:(d + 2) * SLOTS,
                    c * WIDE:c * WIDE + taps,
                ] = both.astype(bf16)
        return carry

    lax.fori_loop(0, slot_total // chunk, gather, 0)

    tap, phase = iota((16, taps), 1), iota((16, taps), 0)
    band = ((tap >= phase) & (tap < phase + length)).astype(bf16)
    lane = iota((PHASES, LANES), 1)

    def correlate(k, carry):
        peer = lax.rem(me + 2 * peers - offset(k), peers)

        @pl.when(k > 0)
        def _():
            transfer(k, peer).wait_recv()

        block = got[peer].astype(f32)

        def windows(j):
            head = block[j * PHASES:(j + 1) * PHASES]
            group = head_rows + j // per_tail * PHASES
            tail = block[group:group + PHASES]
            rows = [head]
            for q in range(1, steps):
                begin = pltpu.roll(head, LANES - q, 1)
                end = pltpu.roll(tail, (LANES - q - steps * (j % per_tail)) % LANES, 1)
                rows.append(jnp.where(lane < LANES - q, begin, end))
            return jnp.concatenate(rows, axis=0).astype(bf16)

        def two_stations(s):
            data = [windows(j) for j in range(s * comps, (s + 2) * comps)]
            squares = jnp.concatenate([x * x for x in data], axis=1)
            data_scale = lax.rsqrt(dot(band, squares)[:PHASES] + epsilon)
            totals = []
            for e in range(2):
                total = None
                for c in range(comps):
                    j = e * comps + c
                    rows = filt[peer * stations + s + e, :, c * WIDE:c * WIDE + taps]
                    product = dot(rows, data[j])
                    start = pl.multiple_of((peer * stations + s + e) * SLOTS, SLOTS)
                    scale = wave_scale[pl.ds(start, SLOTS), c * LANES:(c + 1) * LANES]
                    own = data_scale[:, j * LANES:(j + 1) * LANES]
                    factor = own[:, None, :] * scale[None, :, :]
                    term = product.reshape(PHASES, SLOTS, LANES) * factor
                    total = term if total is None else total + term
                totals.append(total)
            return totals

        for s in range(0, stations, 2):
            low, high = two_stations(s)
            start = pl.multiple_of((peer * stations + s) * SLOTS, 2 * SLOTS)
            for d in range(PHASES):
                scores[pl.ds(start, 2 * SLOTS), d * LANES:(d + 1) * LANES] = jnp.concatenate(
                    [low[d], high[d]], axis=0
                ).astype(bf16)
        return carry

    lax.fori_loop(0, peers, correlate, 0)

    found = dot(combine, scores[...])
    coarse = found.astype(bf16)
    fine = (found - coarse.astype(f32)).astype(bf16)
    out = dot(coarse, order[...]) + dot(fine, order[...])
    out_ref[...] = out[:K_DEV]

    def drain(k, carry):
        transfer(k, me).wait_send()
        return carry

    lax.fori_loop(1, peers, drain, 0)


def per_device(peers, seismo, waves, pair_station, pair_template, chan_mask):
    stations, comps, samples = seismo.shape
    pairs, _, length = waves.shape
    lags = samples - length + 1
    assert lags == PHASES * LANES
    assert 2 * pairs // (stations * peers) <= SLOTS
    slot_total = peers * stations * SLOTS
    steps = -(-(length + PHASES - 1) // 16) * 16 // PHASES
    tail_groups = -(-stations * comps // (LANES // steps))
    rows = -(-(stations * comps + tail_groups) // 2) * 2 * PHASES
    vmem = pl.BlockSpec(memory_space=pltpu.VMEM)
    bf16 = jnp.bfloat16
    return pl.pallas_call(
        functools.partial(kernel, peers, stations, comps, length),
        out_shape=jax.ShapeDtypeStruct((K_DEV, lags), jnp.float32),
        in_specs=[vmem] * 5,
        out_specs=vmem,
        scratch_shapes=[
            pltpu.VMEM((peers, rows, LANES), bf16),
            pltpu.VMEM((PHASES, comps, steps * PHASES, pairs), bf16),
            pltpu.VMEM((slot_total, pairs), bf16),
            pltpu.VMEM((peers * stations, PHASES * SLOTS, comps * WIDE), bf16),
            pltpu.VMEM((slot_total, comps * LANES), jnp.float32),
            pltpu.VMEM((slot_total, lags), bf16),
            pltpu.VMEM((lags, lags), bf16),
            pltpu.SemaphoreType.DMA((peers,)),
            pltpu.SemaphoreType.DMA((peers,)),
        ],
        compiler_params=pltpu.CompilerParams(
            collective_id=0, has_side_effects=True, vmem_limit_bytes=56 * 1024 * 1024
        ),
    )(
        jnp.transpose(seismo, (1, 0, 2)),
        jnp.transpose(waves, (1, 2, 0)),
        pair_station.reshape(1, pairs),
        pair_template.reshape(1, pairs),
        chan_mask,
    )


def solution(mesh):
    return jax.shard_map(
        functools.partial(per_device, mesh.shape["sta"]),
        mesh=mesh,
        in_specs=(
            P(("days", "sta"), None, None),
            P("sta", None, None),
            P("sta", None),
            P("sta"),
            P(("days", "sta"), None),
        ),
        out_specs=P(("days", "sta"), None),
        check_vma=False,
    )
```

```python
import functools

import jax
import jax.numpy as jnp
from jax import lax
from jax.experimental import pallas as pl
from jax.experimental.pallas import tpu as pltpu
from jax.sharding import PartitionSpec as P

K_DEV = 24
SLOTS = 8
PHASES = 8
LANES = 128
WIDE = 256
MESH = pl.DeviceIdType.MESH

epsilon = 1e-06


def dot(a, b):
    return jnp.dot(a, b, preferred_element_type=jnp.float32)


def iota(shape, dim):
    return lax.broadcasted_iota(jnp.int32, shape, dim)


def kernel(
    peers, stations, comps, length,
    seismo_ref, waves_ref, station_ref, template_ref, mask_ref, out_ref,
    got, shifted, chooser, filt, wave_scale, scores, order, send_sem, recv_sem,
):
    f32, bf16 = jnp.float32, jnp.bfloat16
    me = lax.axis_index("sta")
    traces = stations * comps
    samples = seismo_ref.shape[2]
    pairs = waves_ref.shape[2]
    slot_total = peers * stations * SLOTS
    taps = -(-(length + PHASES - 1) // 16) * 16
    steps = taps // PHASES
    per_tail = LANES // steps
    tail_groups = -(-traces // per_tail)
    head_rows = traces * PHASES

    barrier = pltpu.get_barrier_semaphore()

    def greet(i, carry):
        pl.semaphore_signal(
            barrier, inc=1, device_id={"sta": lax.rem(me + i, peers)}, device_id_type=MESH
        )
        return carry

    lax.fori_loop(1, peers, greet, 0)

    spread = None
    for c in range(comps):
        source = iota((head_rows, stations), 0) // PHASES
        pick = (source == iota((head_rows, stations), 1) * comps + c).astype(bf16)
        record = seismo_ref[c].astype(f32) * mask_ref[:, c:c + 1].astype(f32)
        one = dot(pick, record.astype(bf16))
        spread = one if spread is None else spread + one
    same_phase = iota((head_rows, samples), 1) % PHASES == iota((head_rows, samples), 0) % PHASES
    spread = jnp.where(same_phase, spread, 0.0).astype(bf16)
    head_pick = (iota((samples, LANES), 0) // PHASES == iota((samples, LANES), 1)).astype(bf16)
    head = dot(spread, head_pick)
    first = PHASES * LANES
    left = samples - first
    tail_pick = (
        iota((left, LANES), 0) // PHASES == iota((left, LANES), 1) % steps
    ).astype(bf16)
    tails = dot(spread[:, first:], tail_pick)
    place = iota((head_rows, LANES), 0) // PHASES % per_tail == iota((head_rows, LANES), 1) // steps
    tails = jnp.where(place, tails, 0.0)
    parts = [head]
    for g in range(tail_groups):
        part = None
        for j in range(g * per_tail, min(traces, (g + 1) * per_tail)):
            one = tails[j * PHASES:(j + 1) * PHASES]
            part = one if part is None else part + one
        parts.append(part)
    if tail_groups % 2:
        parts.append(jnp.zeros((PHASES, LANES), f32))
    got[me] = jnp.concatenate(parts, axis=0).astype(bf16)

    assert peers & (peers - 1) == 0

    def partner(k):
        total = 0
        bit = 1
        while bit < peers:
            total = total + (me // bit + k // bit) % 2 * bit
            bit *= 2
        return total

    def transfer(k, source):
        return pltpu.make_async_remote_copy(
            src_ref=got.at[source],
            dst_ref=got.at[source],
            send_sem=send_sem.at[k],
            recv_sem=recv_sem.at[source],
            device_id={"sta": partner(k)},
            device_id_type=MESH,
        )

    diagonal = iota((pairs, pairs), 0) == iota((pairs, pairs), 1)
    station_row = station_ref[...]
    station_column = jnp.sum(jnp.where(diagonal, station_row, 0), axis=1, keepdims=True)
    earlier = iota((pairs, pairs), 0) < iota((pairs, pairs), 1)
    matched = (station_column == station_row) & earlier
    rank = jnp.sum(matched.astype(jnp.int32), axis=0, keepdims=True)
    slot = station_row * SLOTS + rank
    chooser[...] = (iota((slot_total, pairs), 0) == slot).astype(bf16)

    for c in range(comps):
        wave = jnp.concatenate(
            [waves_ref[c].astype(f32), jnp.zeros((taps - length, pairs), f32)], axis=0
        )
        for d in range(PHASES):
            moved = wave if d == 0 else pltpu.roll(wave, d, 0)
            shifted[d, c] = moved.astype(bf16)

    lags = PHASES * LANES
    for d in range(PHASES):
        order[d * LANES:(d + 1) * LANES, :] = (
            iota((LANES, lags), 1) == PHASES * iota((LANES, lags), 0) + d
        ).astype(bf16)
    member = (iota((32, pairs), 0) == template_ref[...]).astype(bf16)
    combine = lax.dot_general(
        member, chooser[...], (((1,), (1,)), ((), ())), preferred_element_type=f32
    ).astype(bf16)
    pl.semaphore_wait(barrier, peers - 1)

    def push(k, carry):
        transfer(k, me).start()
        return carry

    lax.fori_loop(1, peers, push, 0)

    chunk = min(2 * pairs, slot_total)
    blocks = chunk // SLOTS

    def gather(i, carry):
        span = pl.ds(pl.multiple_of(i * chunk, chunk), chunk)
        rows = chooser[span, :]
        for c in range(comps):
            for d in range(0, PHASES, 2):
                low, high = [
                    lax.dot_general(
                        rows, shifted[d + e, c], (((1,), (1,)), ((), ())),
                        preferred_element_type=f32,
                    )
                    for e in range(2)
                ]
                if d == 0:
                    energy = jnp.sum(jnp.square(low), axis=1, keepdims=True)
                    wave_scale[span, c * LANES:(c + 1) * LANES] = jnp.broadcast_to(
                        lax.rsqrt(energy + epsilon), (chunk, LANES)
                    )
                both = jnp.concatenate(
                    [low.reshape(blocks, SLOTS, taps), high.reshape(blocks, SLOTS, taps)], axis=1
                )
                filt[
                    pl.ds(i * blocks, blocks), d * SLOTS:(d + 2) * SLOTS,
                    c * WIDE:c * WIDE + taps,
                ] = both.astype(bf16)
        return carry

    lax.fori_loop(0, slot_total // chunk, gather, 0)

    tap, phase = iota((16, taps), 1), iota((16, taps), 0)
    band = ((tap >= phase) & (tap < phase + length)).astype(bf16)
    lane = iota((PHASES, LANES), 1)

    def correlate(k, carry):
        peer = partner(k)

        @pl.when(k > 0)
        def _():
            transfer(k, peer).wait_recv()

        block = got[peer].astype(f32)

        def windows(j):
            head = block[j * PHASES:(j + 1) * PHASES]
            group = head_rows + j // per_tail * PHASES
            tail = block[group:group + PHASES]
            rows = [head]
            for q in range(1, steps):
                begin = pltpu.roll(head, LANES - q, 1)
                end = pltpu.roll(tail, (LANES - q - steps * (j % per_tail)) % LANES, 1)
                rows.append(jnp.where(lane < LANES - q, begin, end))
            return jnp.concatenate(rows, axis=0).astype(bf16)

        def two_stations(s):
            data = [windows(j) for j in range(s * comps, (s + 2) * comps)]
            squares = jnp.concatenate([x * x for x in data], axis=1)
            data_scale = lax.rsqrt(dot(band, squares)[:PHASES] + epsilon)
            totals = []
            for e in range(2):
                total = None
                for c in range(comps):
                    j = e * comps + c
                    rows = filt[peer * stations + s + e, :, c * WIDE:c * WIDE + taps]
                    product = dot(rows, data[j])
                    start = pl.multiple_of((peer * stations + s + e) * SLOTS, SLOTS)
                    scale = wave_scale[pl.ds(start, SLOTS), c * LANES:(c + 1) * LANES]
                    own = data_scale[:, j * LANES:(j + 1) * LANES]
                    factor = own[:, None, :] * scale[None, :, :]
                    term = product.reshape(PHASES, SLOTS, LANES) * factor
                    total = term if total is None else total + term
                totals.append(total)
            return totals

        for s in range(0, stations, 2):
            low, high = two_stations(s)
            start = pl.multiple_of((peer * stations + s) * SLOTS, 2 * SLOTS)
            for d in range(PHASES):
                scores[pl.ds(start, 2 * SLOTS), d * LANES:(d + 1) * LANES] = jnp.concatenate(
                    [low[d], high[d]], axis=0
                ).astype(bf16)
        return carry

    lax.fori_loop(0, peers, correlate, 0)

    found = dot(combine, scores[...])
    coarse = found.astype(bf16)
    fine = (found - coarse.astype(f32)).astype(bf16)
    out = dot(coarse, order[...]) + dot(fine, order[...])
    out_ref[...] = out[:K_DEV]

    def drain(k, carry):
        transfer(k, me).wait_send()
        return carry

    lax.fori_loop(1, peers, drain, 0)


def per_device(peers, seismo, waves, pair_station, pair_template, chan_mask):
    stations, comps, samples = seismo.shape
    pairs, _, length = waves.shape
    lags = samples - length + 1
    assert lags == PHASES * LANES
    assert 2 * pairs // (stations * peers) <= SLOTS
    slot_total = peers * stations * SLOTS
    steps = -(-(length + PHASES - 1) // 16) * 16 // PHASES
    tail_groups = -(-stations * comps // (LANES // steps))
    rows = -(-(stations * comps + tail_groups) // 2) * 2 * PHASES
    vmem = pl.BlockSpec(memory_space=pltpu.VMEM)
    bf16 = jnp.bfloat16
    return pl.pallas_call(
        functools.partial(kernel, peers, stations, comps, length),
        out_shape=jax.ShapeDtypeStruct((K_DEV, lags), jnp.float32),
        in_specs=[vmem] * 5,
        out_specs=vmem,
        scratch_shapes=[
            pltpu.VMEM((peers, rows, LANES), bf16),
            pltpu.VMEM((PHASES, comps, steps * PHASES, pairs), bf16),
            pltpu.VMEM((slot_total, pairs), bf16),
            pltpu.VMEM((peers * stations, PHASES * SLOTS, comps * WIDE), bf16),
            pltpu.VMEM((slot_total, comps * LANES), jnp.float32),
            pltpu.VMEM((slot_total, lags), bf16),
            pltpu.VMEM((lags, lags), bf16),
            pltpu.SemaphoreType.DMA((peers,)),
            pltpu.SemaphoreType.DMA((peers,)),
        ],
        compiler_params=pltpu.CompilerParams(
            collective_id=0, has_side_effects=True, vmem_limit_bytes=56 * 1024 * 1024
        ),
    )(
        jnp.transpose(seismo, (1, 0, 2)),
        jnp.transpose(waves, (1, 2, 0)),
        pair_station.reshape(1, pairs),
        pair_template.reshape(1, pairs),
        chan_mask,
    )


def solution(mesh):
    return jax.shard_map(
        functools.partial(per_device, mesh.shape["sta"]),
        mesh=mesh,
        in_specs=(
            P(("days", "sta"), None, None),
            P("sta", None, None),
            P("sta", None),
            P("sta"),
            P(("days", "sta"), None),
        ),
        out_specs=P(("days", "sta"), None),
        check_vma=False,
    )
```
